32 devices in a mesh: groups: 2 (over y), ckpt: 2 (over x), store: 8 (over z, core).
Axes of the slice: x: 2, y: 2, z: 4, core: 2. Of those that a mesh axis runs over, the one named last changes fastest.
Arguments:
- queries: bfloat16 [2, 768, 2048], P('ckpt', 'groups', 'store'), parts along dimension 1, may hold values from -0.125 to 0.125
- fisher_inv: bfloat16 [2, 2048, 2048], P('ckpt', 'store'), may hold values from -1 to 3, as said below
- slab_feats: bfloat16 [2, 16384, 2048], P('ckpt', ('groups', 'store')), parts along dimension 1, may hold values from -6 to 6
- row_ids: int32 [16384], P(('groups', 'store')), parts along dimension 0, may hold values from 0 to 32767
- resid_weight: float32 [2, 32768], P('ckpt'), may hold values from 0.05 to 1
Outputs:
- scores: float32 [768, 8192], P(('groups', 'ckpt'), 'store'), parts along dimension 0
The draws below stay inside these ranges and needn't reach their ends.
There are 2 independent parts, one for each index of `groups`. The reference program is written for one: setup_inputs(seed, part) draws one part's arguments, and reference() takes and returns one part's arrays. A program takes and returns all parts, laid end to end along the dimension named above; an argument that names none is the same for every part. Nothing has to cross between parts.
Inputs may be any that keep to these rules, and one draw needn't show every extreme that they name: `fisher_inv`: each checkpoint's matrix is symmetric and positive definite.
All inputs are finite; a program needn't handle non-finite values.
Results may differ from the reference program's by a relative error of at most 0.0029.
Values may be sent and summed in bfloat16 or wider, within the bound.
A program may use at most 64 MiB of HBM per device.

```python
import math
import jax
import jax.numpy as jnp
from jax import lax

K = 2048
Q = 384
TABLE = 32768
CKPT = 2
ROWS = 8192


def draw_fisher_inv(key, part):
    key = jax.random.fold_in(key, 7)
    first_key, second_key = jax.random.split(key)
    raw = jax.random.normal(first_key, (CKPT, K, K), jnp.float32)
    offdiag = (raw + jnp.swapaxes(raw, 1, 2)) * (0.5 / (2.0 * K) ** 0.5)
    unit = jnp.eye(K, dtype=jnp.float32)[None, :, :]
    diagonal = jax.random.uniform(second_key, (CKPT, 1, K), jnp.float32, 1.5, 3.0)
    matrix = offdiag * (1.0 - unit) + unit * diagonal
    return jnp.clip(matrix, -1.0, 3.0).astype(jnp.bfloat16)


def with_ends(array, stream_key, smallest, top_value):
    spot = [jax.random.randint(jax.random.fold_in(stream_key, axis), (), 0, length) for axis, length in enumerate(array.shape)]
    main_axis = array.shape.index(max(array.shape))
    beside = spot[:main_axis] + [(spot[main_axis] + 1) % array.shape[main_axis]] + spot[main_axis + 1:]
    return array.at[tuple(spot)].set(smallest).at[tuple(beside)].set(top_value)


def shard_levels(rng, shape, cuts, least, high):
    factor_of, own = 1.0, jax.random.fold_in(rng, 6)
    for position, blocks in cuts:
        steps = jnp.exp(jax.random.uniform(jax.random.fold_in(own, position), (blocks,), jnp.float32, least / len(cuts), high / len(cuts)))
        factor_of = factor_of * jnp.repeat(steps, shape[position] // blocks).reshape([-1 if axis == position else 1 for axis in range(len(shape))])
    return factor_of


def normal_values(rng, shape, spread, reach, cuts=(), kind=jnp.bfloat16):
    result = spread * jax.random.normal(rng, shape, jnp.float32)
    if cuts:
        result = result * shard_levels(rng, shape, cuts, -0.22, 0.18)
    return jnp.clip(result, -reach, reach).astype(kind)


def setup_inputs(seed: int = 0, part: int = 0) -> dict:
    seeds = jax.random.split(jax.random.key(seed), 6)
    part_splits = jax.random.split(jax.random.fold_in(seeds[5], part), 6)
    queries = normal_values(part_splits[0], (CKPT, Q, K), K ** -0.5, 0.125, ((0, 2), (2, 8)))
    fisher_inv = draw_fisher_inv(jax.random.fold_in(seeds[5], 71), part)
    slab_feats = normal_values(part_splits[2], (CKPT, ROWS, K), 1.0, 6.0, ((0, 2), (1, 8)))
    row_ids = with_ends(jax.random.randint(part_splits[3], (ROWS,), 0, TABLE), jax.random.fold_in(part_splits[3], 1), 0, TABLE - 1).astype(jnp.int32)
    resid_weight = jnp.clip(jnp.exp(math.log(1.0) - 2.9957323 * jax.random.uniform(seeds[4], (CKPT, TABLE), jnp.float32) ** shard_levels(seeds[4], (CKPT, TABLE), ((0, 2),), -0.2, 0.2)), 0.05, 1.0)
    return {"queries": queries, "fisher_inv": fisher_inv, "slab_feats": slab_feats, "row_ids": row_ids, "resid_weight": resid_weight}


def reference(queries, fisher_inv, slab_feats, row_ids, resid_weight):
    def step(total, items):
        query_mat, fisher_mat, feats, weight_row = items
        precond = jnp.dot(query_mat, fisher_mat, preferred_element_type=jnp.float32).astype(jnp.bfloat16)
        partial_value = lax.dot_general(precond, feats, (((1,), (1,)), ((), ())), preferred_element_type=jnp.float32)
        weights = jnp.take(weight_row, row_ids, axis=0)
        return total + partial_value * weights[None, :], None

    start_total = jnp.zeros((queries.shape[1], slab_feats.shape[1]), jnp.float32)
    total, unused = lax.scan(step, start_total, (queries, fisher_inv, slab_feats, resid_weight))
    return total * (1.0 / CKPT)
```

```python
import functools

import jax
import jax.numpy as jnp
from jax import lax
from jax.experimental import pallas as pl
from jax.experimental.pallas import tpu as pltpu
from jax.sharding import PartitionSpec as P

MESH = pl.DeviceIdType.MESH
NT = (((1,), (1,)), ((), ()))
TN = (((0,), (0,)), ((), ()))


def plain_body(queries, fisher_inv, slab_feats, row_ids, resid_weight):
    feats = slab_feats[0]
    fisher_rows = fisher_inv[0]
    whole_queries = lax.all_gather(queries[0], "store", axis=1, tiled=True)
    own_cols = lax.dot_general(
        whole_queries, fisher_rows, NT, preferred_element_type=jnp.float32
    ).astype(jnp.bfloat16)
    partial_value = lax.dot_general(
        lax.all_gather(own_cols, "store", axis=1, tiled=True), feats, NT, preferred_element_type=jnp.float32
    )
    weights = jnp.take(resid_weight[0], row_ids, axis=0)
    weighted = partial_value * weights[None, :]
    members = lax.axis_size("ckpt")
    summed = lax.psum_scatter(weighted, "ckpt", scatter_dimension=0, tiled=True)
    return summed * (1.0 / members)


def kernel(
    chips, tiles, q_hbm, f_hbm, s_hbm, id_ref, table_ref, out_ref,
    gathered, fisher, slab, acc, weight, sent, landed, local_sem, send_sem, recv_sem, xsend_sem, xrecv_sem,
):
    g, c, s = lax.axis_index("groups"), lax.axis_index("ckpt"), lax.axis_index("store")
    z, core = s // 2, s % 2
    width = q_hbm.shape[-1]
    cols = out_ref.shape[-1] // tiles

    loads = [
        pltpu.make_async_copy(q_hbm, gathered.at[0, s], local_sem.at[0]),
        pltpu.make_async_copy(f_hbm, fisher, local_sem.at[1]),
        pltpu.make_async_copy(s_hbm, slab, local_sem.at[2]),
    ]
    for load in loads:
        load.start()

    barrier = pltpu.get_barrier_semaphore()

    def greet(cc, ss):
        pl.semaphore_signal(barrier, inc=1, device_id=(g, cc, ss), device_id_type=MESH)

    greet(c, s + 1 - 2 * core)
    greet(1 - c, s)

    @pl.when(z > 0)
    def _():
        greet(c, s - 2)

    @pl.when(z < chips - 1)
    def _():
        greet(c, s + 2)

    pl.semaphore_wait(barrier, 2 + jnp.where(z > 0, 1, 0) + jnp.where(z < chips - 1, 1, 0))

    def copy(phase, way, origin, half, target):
        slot = 2 * origin + core
        return pltpu.make_async_remote_copy(
            src_ref=gathered.at[phase, slot, half],
            dst_ref=gathered.at[phase, slot, half],
            send_sem=send_sem.at[phase, way, origin, half],
            recv_sem=recv_sem.at[phase, slot, half],
            device_id=(g, c, target),
            device_id_type=MESH,
        )

    def arrived(phase, slot, half):
        pltpu.make_async_remote_copy(
            src_ref=gathered.at[phase, slot, half],
            dst_ref=gathered.at[phase, slot, half],
            send_sem=send_sem.at[phase, 0, 0, half],
            recv_sem=recv_sem.at[phase, slot, half],
            device_id=(g, c, s + 1 - 2 * core),
            device_id_type=MESH,
        ).wait_recv()

    def send(phase, origin, half, ways):
        if 0 in ways:
            @pl.when(z > 0)
            def _():
                copy(phase, 0, origin, half, s - 2).start()
        if 1 in ways:
            @pl.when(z < chips - 1)
            def _():
                copy(phase, 1, origin, half, s + 2).start()
        copy(phase, 2, origin, half, s + 1 - 2 * core).start()

    def relay(phase, hop, half):
        @pl.when(z + hop < chips)
        def _():
            arrived(phase, 2 * (z + hop) + core, half)
            send(phase, z + hop, half, (0,))

        @pl.when(z - hop >= 0)
        def _():
            arrived(phase, 2 * (z - hop) + core, half)
            send(phase, z - hop, half, (1,))

    def half_of(j):
        return jnp.where(j == 0, 1 - c, c)

    loads[0].wait()
    for j in range(2):
        send(0, z, half_of(j), (0, 1))

    acc[...] = jnp.zeros_like(acc)
    ids = id_ref[...]
    rows = table_ref.shape[0]
    picked = jnp.where(
        lax.broadcasted_iota(jnp.int32, (rows, ids.shape[1]), 0) == lax.shift_right_logical(ids, 7), 1.0, 0.0
    ).astype(jnp.bfloat16)
    rest = table_ref[...]
    found = jnp.zeros((128, ids.shape[1]), jnp.float32)
    for _ in range(3):
        piece = rest.astype(jnp.bfloat16)
        found = found + lax.dot_general(piece, picked, TN, preferred_element_type=jnp.float32)
        rest = rest - piece.astype(jnp.float32)
    lane = lax.broadcasted_iota(jnp.int32, found.shape, 0)
    weight[...] = jnp.sum(jnp.where(lane == (ids & 127), found, 0.0), axis=0, keepdims=True)

    def relay_query(t, carry):
        relay(0, 1 + t // 2, half_of(t % 2))
        return carry

    def precondition(half):
        def other(o, carry):
            arrived(0, 2 * o + 1 - core, half)
            return carry

        lax.fori_loop(0, chips, other, 0)

        total = jnp.zeros((q_hbm.shape[1], width), jnp.float32)
        for slot in range(2 * chips):
            total = total + lax.dot_general(
                gathered[0, slot, half], fisher[:, slot * width:(slot + 1) * width], NT,
                preferred_element_type=jnp.float32,
            )
        gathered[1, s, half] = total.astype(jnp.bfloat16)
        send(1, z, half, (0, 1))

    last = 2 * (chips - 1) - 1
    lax.fori_loop(0, last, relay_query, 0)
    loads[1].wait()
    precondition(half_of(0))
    lax.fori_loop(last, last + 1, relay_query, 0)
    precondition(half_of(1))
    loads[2].wait()

    def score(slot, half, j):
        at = pl.ds(pl.multiple_of(slot * width, width), width)
        acc[j] += lax.dot_general(
            gathered[1, slot, half], slab[:, at], NT, preferred_element_type=jnp.float32
        )

    def score_step(t, carry):
        hop, j = t // 2, t % 2
        half = half_of(j)

        @pl.when(hop > 0)
        def _():
            relay(1, hop, half)

        def part(e, carry):
            side, other = e % 2, e // 2
            origin = z + hop * (1 - 2 * side)
            slot = 2 * origin + jnp.where(other == 0, core, 1 - core)
            valid = (origin >= 0) & (origin < chips) & ((hop > 0) | (side == 0))

            @pl.when(valid & (other == 1))
            def _():
                arrived(1, slot, half)

            @pl.when(valid)
            def _():
                score(slot, half, j)

            return carry

        return lax.fori_loop(0, 4, part, carry)

    def cross(tile):
        return pltpu.make_async_remote_copy(
            src_ref=sent.at[tile],
            dst_ref=landed.at[tile],
            send_sem=xsend_sem.at[tile],
            recv_sem=xrecv_sem.at[tile],
            device_id=(g, 1 - c, s),
            device_id_type=MESH,
        )

    last = 2 * chips - 1
    lax.fori_loop(0, last, score_step, 0)
    for tile in range(tiles):
        at = slice(tile * cols, (tile + 1) * cols)
        sent[tile] = (acc[0, :, at] * weight[:, at]).astype(jnp.bfloat16)
        cross(tile).start()
    lax.fori_loop(last, last + 1, score_step, 0)
    for tile in range(tiles):
        at = slice(tile * cols, (tile + 1) * cols)
        cross(tile).wait_recv()
        out_ref[:, at] = (acc[1, :, at] * weight[:, at] + landed[tile].astype(jnp.float32)) * 0.5

    def drain(t, carry):
        phase, origin, half = t // (2 * chips), (t // 2) % chips, t % 2
        copy(phase, 2, origin, half, s + 1 - 2 * core).wait_send()

        @pl.when((z > 0) & (origin >= z))
        def _():
            copy(phase, 0, origin, half, s - 2).wait_send()

        @pl.when((z < chips - 1) & (origin <= z))
        def _():
            copy(phase, 1, origin, half, s + 2).wait_send()

        return carry

    lax.fori_loop(0, 4 * chips, drain, 0)
    for tile in range(tiles):
        cross(tile).wait_send()


def fused_body(queries, fisher_inv, slab_feats, row_ids, resid_weight, chips):
    count, width = queries.shape[1:]
    half, rows, depth, tiles = count // 2, slab_feats.shape[1], slab_feats.shape[2], 4
    table = resid_weight.shape[1]
    slots = 2 * chips
    hbm, vmem = pl.BlockSpec(memory_space=pl.ANY), pl.BlockSpec(memory_space=pltpu.VMEM)
    return pl.pallas_call(
        functools.partial(kernel, chips, tiles),
        out_shape=jax.ShapeDtypeStruct((half, rows), jnp.float32),
        in_specs=[hbm, hbm, hbm, vmem, vmem],
        out_specs=vmem,
        scratch_shapes=[
            pltpu.VMEM((2, slots, 2, half, width), jnp.bfloat16),
            pltpu.VMEM((width, depth), jnp.bfloat16),
            pltpu.VMEM((rows, depth), jnp.bfloat16),
            pltpu.VMEM((2, half, rows), jnp.float32),
            pltpu.VMEM((1, rows), jnp.float32),
            pltpu.VMEM((tiles, half, rows // tiles), jnp.bfloat16),
            pltpu.VMEM((tiles, half, rows // tiles), jnp.bfloat16),
            pltpu.SemaphoreType.DMA((3,)),
            pltpu.SemaphoreType.DMA((2, 3, chips, 2)),
            pltpu.SemaphoreType.DMA((2, slots, 2)),
            pltpu.SemaphoreType.DMA((tiles,)),
            pltpu.SemaphoreType.DMA((tiles,)),
        ],
        compiler_params=pltpu.CompilerParams(
            collective_id=0, has_side_effects=True, vmem_limit_bytes=40 * 1024 * 1024
        ),
        cost_estimate=pl.CostEstimate(
            flops=2 * count * depth * (width + rows), bytes_accessed=2 * depth * (width + rows), transcendentals=0
        ),
    )(
        queries.reshape(2, half, width),
        fisher_inv[0],
        slab_feats[0],
        row_ids.reshape(1, rows),
        resid_weight.reshape(table // 128, 128),
    )


def solution(mesh):
    placed = (
        P("ckpt", "groups", "store"),
        P("ckpt", "store", None),
        P("ckpt", ("groups", "store"), None),
        P(("groups", "store")),
        P("ckpt", None),
    )
    body = plain_body
    if mesh.shape["ckpt"] == 2 and mesh.shape["store"] == 8:
        body = functools.partial(fused_body, chips=mesh.shape["store"] // 2)
    return jax.shard_map(
        body, mesh=mesh, in_specs=placed, out_specs=P(("groups", "ckpt"), "store"), check_vma=False
    )
```

```python
import functools

import jax
import jax.numpy as jnp
from jax import lax
from jax.experimental import pallas as pl
from jax.experimental.pallas import tpu as pltpu
from jax.sharding import PartitionSpec as P

MESH = pl.DeviceIdType.MESH
NT = (((1,), (1,)), ((), ()))
TN = (((0,), (0,)), ((), ()))


def plain_body(queries, fisher_inv, slab_feats, row_ids, resid_weight):
    feats = slab_feats[0]
    fisher_rows = fisher_inv[0]
    whole_queries = lax.all_gather(queries[0], "store", axis=1, tiled=True)
    own_cols = lax.dot_general(
        whole_queries, fisher_rows, NT, preferred_element_type=jnp.float32
    ).astype(jnp.bfloat16)
    partial_value = lax.dot_general(
        lax.all_gather(own_cols, "store", axis=1, tiled=True), feats, NT, preferred_element_type=jnp.float32
    )
    weights = jnp.take(resid_weight[0], row_ids, axis=0)
    weighted = partial_value * weights[None, :]
    members = lax.axis_size("ckpt")
    summed = lax.psum_scatter(weighted, "ckpt", scatter_dimension=0, tiled=True)
    return summed * (1.0 / members)


def kernel(
    chips, tiles, q_hbm, f_hbm, s_hbm, id_hbm, table_hbm, out_ref,
    id_ref, table_ref, gathered, fisher, slab, acc, weight, sent, landed, local_sem, send_sem, recv_sem, xsend_sem, xrecv_sem,
):
    g, c, s = lax.axis_index("groups"), lax.axis_index("ckpt"), lax.axis_index("store")
    z, core = s // 2, s % 2
    width = q_hbm.shape[-1]
    cols = out_ref.shape[-1] // tiles

    loads = [
        pltpu.make_async_copy(q_hbm, gathered.at[0, s], local_sem.at[0]),
        pltpu.make_async_copy(f_hbm, fisher, local_sem.at[1]),
        pltpu.make_async_copy(id_hbm, id_ref, local_sem.at[3]),
        pltpu.make_async_copy(table_hbm, table_ref, local_sem.at[4]),
        pltpu.make_async_copy(s_hbm, slab, local_sem.at[2]),
    ]
    for load in loads:
        load.start()

    barrier = pltpu.get_barrier_semaphore()

    def greet(cc, ss):
        pl.semaphore_signal(barrier, inc=1, device_id=(g, cc, ss), device_id_type=MESH)

    greet(c, s + 1 - 2 * core)
    greet(1 - c, s)

    @pl.when(z > 0)
    def _():
        greet(c, s - 2)

    @pl.when(z < chips - 1)
    def _():
        greet(c, s + 2)

    pl.semaphore_wait(barrier, 2 + jnp.where(z > 0, 1, 0) + jnp.where(z < chips - 1, 1, 0))

    def copy(phase, way, origin, half, target):
        slot = 2 * origin + core
        return pltpu.make_async_remote_copy(
            src_ref=gathered.at[phase, slot, half],
            dst_ref=gathered.at[phase, slot, half],
            send_sem=send_sem.at[phase, way, origin, half],
            recv_sem=recv_sem.at[phase, slot, half],
            device_id=(g, c, target),
            device_id_type=MESH,
        )

    def arrived(phase, slot, half):
        pltpu.make_async_remote_copy(
            src_ref=gathered.at[phase, slot, half],
            dst_ref=gathered.at[phase, slot, half],
            send_sem=send_sem.at[phase, 0, 0, half],
            recv_sem=recv_sem.at[phase, slot, half],
            device_id=(g, c, s + 1 - 2 * core),
            device_id_type=MESH,
        ).wait_recv()

    def send(phase, origin, half, ways):
        if 0 in ways:
            @pl.when(z > 0)
            def _():
                copy(phase, 0, origin, half, s - 2).start()
        if 1 in ways:
            @pl.when(z < chips - 1)
            def _():
                copy(phase, 1, origin, half, s + 2).start()
        copy(phase, 2, origin, half, s + 1 - 2 * core).start()

    def relay(phase, hop, half):
        @pl.when(z + hop < chips)
        def _():
            arrived(phase, 2 * (z + hop) + core, half)
            send(phase, z + hop, half, (0,))

        @pl.when(z - hop >= 0)
        def _():
            arrived(phase, 2 * (z - hop) + core, half)
            send(phase, z - hop, half, (1,))

    def half_of(j):
        return jnp.where(j == 0, 1 - c, c)

    loads[0].wait()
    for j in range(2):
        send(0, z, half_of(j), (0, 1))

    acc[...] = jnp.zeros_like(acc)
    loads[2].wait()
    loads[3].wait()
    ids = id_ref[...]
    rows = table_ref.shape[0]
    picked = jnp.where(
        lax.broadcasted_iota(jnp.int32, (rows, ids.shape[1]), 0) == lax.shift_right_logical(ids, 7), 1.0, 0.0
    ).astype(jnp.bfloat16)
    rest = table_ref[...]
    found = jnp.zeros((128, ids.shape[1]), jnp.float32)
    for _ in range(3):
        piece = rest.astype(jnp.bfloat16)
        found = found + lax.dot_general(piece, picked, TN, preferred_element_type=jnp.float32)
        rest = rest - piece.astype(jnp.float32)
    lane = lax.broadcasted_iota(jnp.int32, found.shape, 0)
    weight[...] = jnp.sum(jnp.where(lane == (ids & 127), found, 0.0), axis=0, keepdims=True)

    def relay_query(t, carry):
        relay(0, 1 + t // 2, half_of(t % 2))
        return carry

    def precondition(half):
        def other(o, carry):
            arrived(0, 2 * o + 1 - core, half)
            return carry

        lax.fori_loop(0, chips, other, 0)

        total = jnp.zeros((q_hbm.shape[1], width), jnp.float32)
        for slot in range(2 * chips):
            total = total + lax.dot_general(
                gathered[0, slot, half], fisher[:, slot * width:(slot + 1) * width], NT,
                preferred_element_type=jnp.float32,
            )
        gathered[1, s, half] = total.astype(jnp.bfloat16)
        send(1, z, half, (0, 1))

    last = 2 * (chips - 1) - 1
    lax.fori_loop(0, last, relay_query, 0)
    loads[1].wait()
    precondition(half_of(0))
    lax.fori_loop(last, last + 1, relay_query, 0)
    precondition(half_of(1))
    loads[4].wait()

    def score(slot, half, j):
        at = pl.ds(pl.multiple_of(slot * width, width), width)
        acc[j] += lax.dot_general(
            gathered[1, slot, half], slab[:, at], NT, preferred_element_type=jnp.float32
        )

    def score_step(t, carry):
        hop, j = t // 2, t % 2
        half = half_of(j)

        @pl.when(hop > 0)
        def _():
            relay(1, hop, half)

        def part(e, carry):
            side, other = e % 2, e // 2
            origin = z + hop * (1 - 2 * side)
            slot = 2 * origin + jnp.where(other == 0, core, 1 - core)
            valid = (origin >= 0) & (origin < chips) & ((hop > 0) | (side == 0))

            @pl.when(valid & (other == 1))
            def _():
                arrived(1, slot, half)

            @pl.when(valid)
            def _():
                score(slot, half, j)

            return carry

        return lax.fori_loop(0, 4, part, carry)

    def cross(tile):
        return pltpu.make_async_remote_copy(
            src_ref=sent.at[tile],
            dst_ref=landed.at[tile],
            send_sem=xsend_sem.at[tile],
            recv_sem=xrecv_sem.at[tile],
            device_id=(g, 1 - c, s),
            device_id_type=MESH,
        )

    last = 2 * chips - 1
    lax.fori_loop(0, last, score_step, 0)
    for tile in range(tiles):
        at = slice(tile * cols, (tile + 1) * cols)
        sent[tile] = (acc[0, :, at] * weight[:, at]).astype(jnp.bfloat16)
        cross(tile).start()
    lax.fori_loop(last, last + 1, score_step, 0)
    for tile in range(tiles):
        at = slice(tile * cols, (tile + 1) * cols)
        cross(tile).wait_recv()
        out_ref[:, at] = (acc[1, :, at] * weight[:, at] + landed[tile].astype(jnp.float32)) * 0.5

    def drain(t, carry):
        phase, origin, half = t // (2 * chips), (t // 2) % chips, t % 2
        copy(phase, 2, origin, half, s + 1 - 2 * core).wait_send()

        @pl.when((z > 0) & (origin >= z))
        def _():
            copy(phase, 0, origin, half, s - 2).wait_send()

        @pl.when((z < chips - 1) & (origin <= z))
        def _():
            copy(phase, 1, origin, half, s + 2).wait_send()

        return carry

    lax.fori_loop(0, 4 * chips, drain, 0)
    for tile in range(tiles):
        cross(tile).wait_send()


def fused_body(queries, fisher_inv, slab_feats, row_ids, resid_weight, chips):
    count, width = queries.shape[1:]
    half, rows, depth, tiles = count // 2, slab_feats.shape[1], slab_feats.shape[2], 4
    table = resid_weight.shape[1]
    slots = 2 * chips
    hbm, vmem = pl.BlockSpec(memory_space=pl.ANY), pl.BlockSpec(memory_space=pltpu.VMEM)
    return pl.pallas_call(
        functools.partial(kernel, chips, tiles),
        out_shape=jax.ShapeDtypeStruct((half, rows), jnp.float32),
        in_specs=[hbm, hbm, hbm, hbm, hbm],
        out_specs=vmem,
        scratch_shapes=[
            pltpu.VMEM((1, rows), jnp.int32),
            pltpu.VMEM((table // 128, 128), jnp.float32),
            pltpu.VMEM((2, slots, 2, half, width), jnp.bfloat16),
            pltpu.VMEM((width, depth), jnp.bfloat16),
            pltpu.VMEM((rows, depth), jnp.bfloat16),
            pltpu.VMEM((2, half, rows), jnp.float32),
            pltpu.VMEM((1, rows), jnp.float32),
            pltpu.VMEM((tiles, half, rows // tiles), jnp.bfloat16),
            pltpu.VMEM((tiles, half, rows // tiles), jnp.bfloat16),
            pltpu.SemaphoreType.DMA((5,)),
            pltpu.SemaphoreType.DMA((2, 3, chips, 2)),
            pltpu.SemaphoreType.DMA((2, slots, 2)),
            pltpu.SemaphoreType.DMA((tiles,)),
            pltpu.SemaphoreType.DMA((tiles,)),
        ],
        compiler_params=pltpu.CompilerParams(
            collective_id=0, has_side_effects=True, vmem_limit_bytes=60 * 1024 * 1024
        ),
        cost_estimate=pl.CostEstimate(
            flops=2 * count * depth * (width + rows), bytes_accessed=2 * depth * (width + rows), transcendentals=0
        ),
    )(
        queries.reshape(2, half, width),
        fisher_inv[0],
        slab_feats[0],
        row_ids.reshape(1, rows),
        resid_weight.reshape(table // 128, 128),
    )


def solution(mesh):
    placed = (
        P("ckpt", "groups", "store"),
        P("ckpt", "store", None),
        P("ckpt", ("groups", "store"), None),
        P(("groups", "store")),
        P("ckpt", None),
    )
    body = plain_body
    if mesh.shape["ckpt"] == 2 and mesh.shape["store"] == 8:
        body = functools.partial(fused_body, chips=mesh.shape["store"] // 2)
    return jax.shard_map(
        body, mesh=mesh, in_specs=placed, out_specs=P(("groups", "ckpt"), "store"), check_vma=False
    )
```

```python
import functools

import jax
import jax.numpy as jnp
from jax import lax
from jax.experimental import pallas as pl
from jax.experimental.pallas import tpu as pltpu
from jax.sharding import PartitionSpec as P

MESH = pl.DeviceIdType.MESH
NT = (((1,), (1,)), ((), ()))
TN = (((0,), (0,)), ((), ()))
PARTS = 2
PLAN = (
    ("send", 0),
    ("send", 1),
    ("send", 2),
    ("send", 3),
    None,
    ("query", 0, 1),
    ("query", 1, 1),
    ("query", 0, 2),
    ("query", 1, 2),
    ("query", 2, 1),
    ("query", 3, 1),
    ("query", 0, 3),
    ("query", 1, 3),
    ("multiply", 0),
    ("multiply", 1),
    ("query", 2, 2),
    ("query", 3, 2),
    ("relay", 0, 1),
    ("relay", 1, 1),
    ("query", 2, 3),
    ("query", 3, 3),
    ("multiply", 2),
    ("multiply", 3),
    ("relay", 0, 2),
    ("relay", 1, 2),
    ("relay", 0, 3),
    ("relay", 1, 3),
    ("relay", 2, 1),
    ("relay", 3, 1),
    ("score", 0),
    ("score", 1),
    ("relay", 2, 2),
    ("relay", 3, 2),
    ("relay", 2, 3),
    ("relay", 3, 3),
    ("score", 2),
    ("score", 3),
)


def plain_body(queries, fisher_inv, slab_feats, row_ids, resid_weight):
    feats = slab_feats[0]
    fisher_rows = fisher_inv[0]
    whole_queries = lax.all_gather(queries[0], "store", axis=1, tiled=True)
    own_cols = lax.dot_general(
        whole_queries, fisher_rows, NT, preferred_element_type=jnp.float32
    ).astype(jnp.bfloat16)
    partial_value = lax.dot_general(
        lax.all_gather(own_cols, "store", axis=1, tiled=True), feats, NT, preferred_element_type=jnp.float32
    )
    weights = jnp.take(resid_weight[0], row_ids, axis=0)
    weighted = partial_value * weights[None, :]
    members = lax.axis_size("ckpt")
    summed = lax.psum_scatter(weighted, "ckpt", scatter_dimension=0, tiled=True)
    return summed * (1.0 / members)


def kernel(
    tiles, parts, q_hbm, f_hbm, s_hbm, id_hbm, table_hbm, out_ref,
    id_ref, table_ref, gathered, fisher, slab, weight, sent, landed,
    local_sem, send_sem, core_sem, recv_sem, xsend_sem, xrecv_sem,
):
    g, c, s = lax.axis_index("groups"), lax.axis_index("ckpt"), lax.axis_index("store")
    z, core = s // 2, s % 2
    inner = (z == 1) | (z == 2)
    outer = jnp.where(z < 2, 0, 3)
    near = jnp.where((z == 0) | (z == 2), 1, 2)
    far = jnp.where(inner, outer, 3 - z)
    third = (z + 2) % 4
    count, width = q_hbm.shape[1:]
    cols = out_ref.shape[-1] // tiles

    loads = [
        pltpu.make_async_copy(q_hbm, gathered.at[0, s], local_sem.at[0]),
        pltpu.make_async_copy(f_hbm, fisher, local_sem.at[1]),
        pltpu.make_async_copy(id_hbm, id_ref, local_sem.at[2]),
        pltpu.make_async_copy(table_hbm, table_ref, local_sem.at[3]),
        pltpu.make_async_copy(s_hbm, slab, local_sem.at[4]),
    ]
    for load in loads:
        load.start()

    barrier = pltpu.get_barrier_semaphore()

    def greet(cc, ss):
        pl.semaphore_signal(barrier, inc=1, device_id=(g, cc, ss), device_id_type=MESH)

    greet(c, s + 1 - 2 * core)
    greet(1 - c, s)

    for d in (1, 2, 3):
        greet(c, 2 * ((z + d) % 4) + core)
    pl.semaphore_wait(barrier, 5)

    def copy(phase, slot, chunk, target, sem):
        return pltpu.make_async_remote_copy(
            src_ref=gathered.at[phase, slot, chunk],
            dst_ref=gathered.at[phase, slot, chunk],
            send_sem=sem,
            recv_sem=recv_sem.at[phase, slot, chunk],
            device_id=(g, c, target),
            device_id_type=MESH,
        )

    def along(phase, origin, chunk, way):
        return copy(phase, 2 * origin + core, chunk, s - 2 + 4 * way, send_sem.at[phase, way, origin, chunk])

    def across(phase, origin, chunk):
        return copy(phase, 2 * origin + core, chunk, s + 1 - 2 * core, core_sem.at[phase, origin, chunk])

    def arrived(phase, slot, chunk):
        copy(phase, slot, chunk, s + 1 - 2 * core, core_sem.at[phase, 0, chunk]).wait_recv()

    def send(phase, chunk):
        @pl.when(z > 0)
        def _():
            along(phase, z, chunk, 0).start()

        @pl.when(z < 3)
        def _():
            along(phase, z, chunk, 1).start()

        across(phase, z, chunk).start()

    def relay(phase, hop, chunk):
        @pl.when(z + hop < 4)
        def _():
            arrived(phase, 2 * (z + hop) + core, chunk)

            @pl.when(z > 0)
            def _():
                along(phase, z + hop, chunk, 0).start()

            across(phase, z + hop, chunk).start()

        @pl.when(z - hop >= 0)
        def _():
            arrived(phase, 2 * (z - hop) + core, chunk)

            @pl.when(z < 3)
            def _():
                along(phase, z - hop, chunk, 1).start()

            across(phase, z - hop, chunk).start()

    def straight(chunk, dest):
        return copy(1, s, chunk, 2 * dest + core, send_sem.at[1, 0, dest, chunk])

    def passed(chunk):
        return copy(1, 2 * near + core, chunk, 2 * outer + core, send_sem.at[1, 1, 0, chunk])

    def send_straight(chunk):
        @pl.when(inner)
        def _():
            straight(chunk, near).start()
            straight(chunk, outer).start()

        @pl.when(jnp.logical_not(inner))
        def _():
            straight(chunk, far).start()
            straight(chunk, third).start()
            straight(chunk, near).start()

        across(1, z, chunk).start()

    def receive(step, chunk):
        origin = (near, far, third)[step - 1]
        arrived(1, 2 * origin + core, chunk)
        if step == 1:
            @pl.when(inner)
            def _():
                passed(chunk).start()

        across(1, origin, chunk).start()

    def other_core(phase, chunk):
        for origin in range(4):
            arrived(phase, 2 * origin + 1 - core, chunk)

    def chunk_of(j):
        return jnp.where(j < parts, (1 - c) * parts + j, c * parts + j - parts)

    loads[0].wait()

    begin = PLAN.index(None)
    for what, j, *rest in PLAN[:begin]:
        send(0, chunk_of(j))

    loads[2].wait()
    loads[3].wait()
    ids = id_ref[...]
    rows = table_ref.shape[0]
    picked = jnp.where(
        lax.broadcasted_iota(jnp.int32, (rows, ids.shape[1]), 0) == lax.shift_right_logical(ids, 7), 1.0, 0.0
    ).astype(jnp.bfloat16)
    rest = table_ref[...]
    found = jnp.zeros((128, ids.shape[1]), jnp.float32)
    for _ in range(3):
        piece = rest.astype(jnp.bfloat16)
        found = found + lax.dot_general(piece, picked, TN, preferred_element_type=jnp.float32)
        rest = rest - piece.astype(jnp.float32)
    lane = lax.broadcasted_iota(jnp.int32, found.shape, 0)
    weight[...] = jnp.sum(jnp.where(lane == (ids & 127), found, 0.0), axis=0, keepdims=True)
    loads[1].wait()

    def precondition(j):
        chunk = chunk_of(j)
        other_core(0, chunk)
        total = jnp.zeros((count, width), jnp.float32)
        for slot in range(8):
            total = total + lax.dot_general(
                gathered[0, slot, chunk], fisher[:, slot * width:(slot + 1) * width], NT,
                preferred_element_type=jnp.float32,
            )
        gathered[1, s, chunk] = total.astype(jnp.bfloat16)
        send_straight(chunk)

    def cross(part, tile):
        return pltpu.make_async_remote_copy(
            src_ref=sent.at[part, tile],
            dst_ref=landed.at[part, tile],
            send_sem=xsend_sem.at[part, tile],
            recv_sem=xrecv_sem.at[part, tile],
            device_id=(g, 1 - c, s),
            device_id_type=MESH,
        )

    def score(chunk, tile):
        total = jnp.zeros((count, cols), jnp.float32)
        for slot in range(8):
            total = total + lax.dot_general(
                gathered[1, slot, chunk], slab[tile * cols:(tile + 1) * cols, slot * width:(slot + 1) * width], NT,
                preferred_element_type=jnp.float32,
            )
        return total * weight[:, tile * cols:(tile + 1) * cols]

    def give(j):
        other_core(1, chunk_of(j))
        for tile in range(tiles):
            sent[j, tile] = score(chunk_of(j), tile).astype(jnp.bfloat16)
            cross(j, tile).start()

    def keep(j):
        other_core(1, chunk_of(j))
        at = slice((j - parts) * count, (j - parts + 1) * count)
        for tile in range(tiles):
            out_ref[at, tile * cols:(tile + 1) * cols] = score(chunk_of(j), tile)

    def add(j, carry):
        at = pl.ds(pl.multiple_of(j * count, count), count)
        for tile in range(tiles):
            cross(j, tile).wait_recv()
            spot = slice(tile * cols, (tile + 1) * cols)
            out_ref[at, spot] = (out_ref[at, spot] + landed[j, tile].astype(jnp.float32)) * 0.5
        return carry

    slab_here = False
    for what, j, *rest in PLAN[begin + 1:]:
        if what == "send":
            send(0, chunk_of(j))
        elif what == "query":
            relay(0, rest[0], chunk_of(j))
        elif what == "multiply":
            precondition(j)
        elif what == "relay":
            receive(rest[0], chunk_of(j))
        else:
            if not slab_here:
                loads[4].wait()
                slab_here = True
            give(j) if j < parts else keep(j)
    lax.fori_loop(0, parts, add, 0)

    def drain(t, carry):
        phase, chunk = t // (2 * parts), t % (2 * parts)

        for origin in range(4):
            across(phase, origin, chunk).wait_send()

            @pl.when((phase == 0) & (z > 0) & (origin >= z))
            def _():
                along(0, origin, chunk, 0).wait_send()

            @pl.when((phase == 0) & (z < 3) & (origin <= z))
            def _():
                along(0, origin, chunk, 1).wait_send()

        @pl.when((phase == 1) & inner)
        def _():
            straight(chunk, near).wait_send()
            straight(chunk, outer).wait_send()
            passed(chunk).wait_send()

        @pl.when((phase == 1) & jnp.logical_not(inner))
        def _():
            for dest in (far, third, near):
                straight(chunk, dest).wait_send()

        return carry

    lax.fori_loop(0, 4 * parts, drain, 0)
    for j in range(parts):
        for tile in range(tiles):
            cross(j, tile).wait_send()


def fused_body(queries, fisher_inv, slab_feats, row_ids, resid_weight):
    whole, width = queries.shape[1:]
    rows, depth, tiles, parts = slab_feats.shape[1], slab_feats.shape[2], 4, PARTS
    count = whole // (2 * parts)
    table = resid_weight.shape[1]
    hbm, vmem = pl.BlockSpec(memory_space=pl.ANY), pl.BlockSpec(memory_space=pltpu.VMEM)
    return pl.pallas_call(
        functools.partial(kernel, tiles, parts),
        out_shape=jax.ShapeDtypeStruct((whole // 2, rows), jnp.float32),
        in_specs=[hbm, hbm, hbm, hbm, hbm],
        out_specs=vmem,
        scratch_shapes=[
            pltpu.VMEM((1, rows), jnp.int32),
            pltpu.VMEM((table // 128, 128), jnp.float32),
            pltpu.VMEM((2, 8, 2 * parts, count, width), jnp.bfloat16),
            pltpu.VMEM((width, depth), jnp.bfloat16),
            pltpu.VMEM((rows, depth), jnp.bfloat16),
            pltpu.VMEM((1, rows), jnp.float32),
            pltpu.VMEM((parts, tiles, count, rows // tiles), jnp.bfloat16),
            pltpu.VMEM((parts, tiles, count, rows // tiles), jnp.bfloat16),
            pltpu.SemaphoreType.DMA((5,)),
            pltpu.SemaphoreType.DMA((2, 2, 4, 2 * parts)),
            pltpu.SemaphoreType.DMA((2, 4, 2 * parts)),
            pltpu.SemaphoreType.DMA((2, 8, 2 * parts)),
            pltpu.SemaphoreType.DMA((parts, tiles)),
            pltpu.SemaphoreType.DMA((parts, tiles)),
        ],
        compiler_params=pltpu.CompilerParams(
            collective_id=0, has_side_effects=True, vmem_limit_bytes=60 * 1024 * 1024
        ),
        cost_estimate=pl.CostEstimate(
            flops=2 * whole * depth * (width + rows), bytes_accessed=2 * depth * (width + rows), transcendentals=0
        ),
    )(
        queries.reshape(2 * parts, count, width),
        fisher_inv[0],
        slab_feats[0],
        row_ids.reshape(1, rows),
        resid_weight.reshape(table // 128, 128),
    )


def solution(mesh):
    placed = (
        P("ckpt", "groups", "store"),
        P("ckpt", "store", None),
        P("ckpt", ("groups", "store"), None),
        P(("groups", "store")),
        P("ckpt", None),
    )
    body = plain_body
    if mesh.shape["ckpt"] == 2 and mesh.shape["store"] == 8:
        body = fused_body
    return jax.shard_map(
        body, mesh=mesh, in_specs=placed, out_specs=P(("groups", "ckpt"), "store"), check_vma=False
    )
```

```python
import functools

import jax
import jax.numpy as jnp
from jax import lax
from jax.experimental import pallas as pl
from jax.experimental.pallas import tpu as pltpu
from jax.sharding import PartitionSpec as P

MESH = pl.DeviceIdType.MESH
NT = (((1,), (1,)), ((), ()))
TN = (((0,), (0,)), ((), ()))
PARTS = 2
PLAN = (
    ("send", 0),
    ("send", 1),
    ("send", 2),
    ("send", 3),
    None,
    ("query", 0, 1),
    ("query", 1, 1),
    ("query", 0, 2),
    ("query", 1, 2),
    ("query", 2, 1),
    ("query", 3, 1),
    ("query", 0, 3),
    ("query", 1, 3),
    ("multiply", 0),
    ("multiply", 1),
    ("query", 2, 2),
    ("query", 3, 2),
    ("relay", 0, 1),
    ("relay", 1, 1),
    ("query", 2, 3),
    ("query", 3, 3),
    ("multiply", 2),
    ("multiply", 3),
    ("relay", 0, 2),
    ("relay", 0, 3),
    ("score", 0),
    ("relay", 1, 2),
    ("relay", 1, 3),
    ("score", 1),
    ("relay", 2, 1),
    ("relay", 3, 1),
    ("relay", 2, 2),
    ("relay", 2, 3),
    ("relay", 3, 2),
    ("relay", 3, 3),
    ("score", 2),
    ("score", 3),
)


def plain_body(queries, fisher_inv, slab_feats, row_ids, resid_weight):
    feats = slab_feats[0]
    fisher_rows = fisher_inv[0]
    whole_queries = lax.all_gather(queries[0], "store", axis=1, tiled=True)
    own_cols = lax.dot_general(
        whole_queries, fisher_rows, NT, preferred_element_type=jnp.float32
    ).astype(jnp.bfloat16)
    partial_value = lax.dot_general(
        lax.all_gather(own_cols, "store", axis=1, tiled=True), feats, NT, preferred_element_type=jnp.float32
    )
    weights = jnp.take(resid_weight[0], row_ids, axis=0)
    weighted = partial_value * weights[None, :]
    members = lax.axis_size("ckpt")
    summed = lax.psum_scatter(weighted, "ckpt", scatter_dimension=0, tiled=True)
    return summed * (1.0 / members)


def kernel(
    tiles, parts, q_hbm, f_hbm, s_hbm, id_hbm, table_hbm, out_ref,
    id_ref, table_ref, gathered, fisher, slab, weight, sent, landed,
    local_sem, send_sem, core_sem, recv_sem, xsend_sem, xrecv_sem,
):
    g, c, s = lax.axis_index("groups"), lax.axis_index("ckpt"), lax.axis_index("store")
    z, core = s // 2, s % 2
    inner = (z == 1) | (z == 2)
    outer = jnp.where(z < 2, 0, 3)
    near = jnp.where((z == 0) | (z == 2), 1, 2)
    far = jnp.where(inner, outer, 3 - z)
    third = (z + 2) % 4
    count, width = q_hbm.shape[1:]
    cols = out_ref.shape[-1] // tiles

    loads = [
        pltpu.make_async_copy(q_hbm, gathered.at[0, s], local_sem.at[0]),
        pltpu.make_async_copy(f_hbm, fisher, local_sem.at[1]),
        pltpu.make_async_copy(id_hbm, id_ref, local_sem.at[2]),
        pltpu.make_async_copy(table_hbm, table_ref, local_sem.at[3]),
        pltpu.make_async_copy(s_hbm, slab, local_sem.at[4]),
    ]
    for load in loads:
        load.start()

    barrier = pltpu.get_barrier_semaphore()

    def greet(cc, ss):
        pl.semaphore_signal(barrier, inc=1, device_id=(g, cc, ss), device_id_type=MESH)

    greet(c, s + 1 - 2 * core)
    greet(1 - c, s)

    for d in (1, 2, 3):
        greet(c, 2 * ((z + d) % 4) + core)
    pl.semaphore_wait(barrier, 5)

    def copy(phase, slot, chunk, target, sem):
        return pltpu.make_async_remote_copy(
            src_ref=gathered.at[phase, slot, chunk],
            dst_ref=gathered.at[phase, slot, chunk],
            send_sem=sem,
            recv_sem=recv_sem.at[phase, slot, chunk],
            device_id=(g, c, target),
            device_id_type=MESH,
        )

    def along(phase, origin, chunk, way):
        return copy(phase, 2 * origin + core, chunk, s - 2 + 4 * way, send_sem.at[phase, way, origin, chunk])

    def across(phase, origin, chunk):
        return copy(phase, 2 * origin + core, chunk, s + 1 - 2 * core, core_sem.at[phase, origin, chunk])

    def arrived(phase, slot, chunk):
        copy(phase, slot, chunk, s + 1 - 2 * core, core_sem.at[phase, 0, chunk]).wait_recv()

    def send(phase, chunk):
        @pl.when(z > 0)
        def _():
            along(phase, z, chunk, 0).start()

        @pl.when(z < 3)
        def _():
            along(phase, z, chunk, 1).start()

        across(phase, z, chunk).start()

    def relay(phase, hop, chunk):
        @pl.when(z + hop < 4)
        def _():
            arrived(phase, 2 * (z + hop) + core, chunk)

            @pl.when(z > 0)
            def _():
                along(phase, z + hop, chunk, 0).start()

            across(phase, z + hop, chunk).start()

        @pl.when(z - hop >= 0)
        def _():
            arrived(phase, 2 * (z - hop) + core, chunk)

            @pl.when(z < 3)
            def _():
                along(phase, z - hop, chunk, 1).start()

            across(phase, z - hop, chunk).start()

    def straight(chunk, dest):
        return copy(1, s, chunk, 2 * dest + core, send_sem.at[1, 0, dest, chunk])

    def passed(chunk):
        return copy(1, 2 * near + core, chunk, 2 * outer + core, send_sem.at[1, 1, 0, chunk])

    def send_straight(chunk):
        @pl.when(inner)
        def _():
            straight(chunk, near).start()
            straight(chunk, outer).start()

        @pl.when(jnp.logical_not(inner))
        def _():
            straight(chunk, far).start()
            straight(chunk, third).start()
            straight(chunk, near).start()

        across(1, z, chunk).start()

    def receive(step, chunk):
        origin = (near, far, third)[step - 1]
        arrived(1, 2 * origin + core, chunk)
        if step == 1:
            @pl.when(inner)
            def _():
                passed(chunk).start()

        across(1, origin, chunk).start()

    def other_core(phase, chunk):
        for origin in range(4):
            arrived(phase, 2 * origin + 1 - core, chunk)

    def chunk_of(j):
        return jnp.where(j < parts, (1 - c) * parts + j, c * parts + j - parts)

    loads[0].wait()

    begin = PLAN.index(None)
    for what, j, *rest in PLAN[:begin]:
        send(0, chunk_of(j))

    loads[2].wait()
    loads[3].wait()
    ids = id_ref[...]
    rows = table_ref.shape[0]
    picked = jnp.where(
        lax.broadcasted_iota(jnp.int32, (rows, ids.shape[1]), 0) == lax.shift_right_logical(ids, 7), 1.0, 0.0
    ).astype(jnp.bfloat16)
    rest = table_ref[...]
    found = jnp.zeros((128, ids.shape[1]), jnp.float32)
    for _ in range(3):
        piece = rest.astype(jnp.bfloat16)
        found = found + lax.dot_general(piece, picked, TN, preferred_element_type=jnp.float32)
        rest = rest - piece.astype(jnp.float32)
    lane = lax.broadcasted_iota(jnp.int32, found.shape, 0)
    weight[...] = jnp.sum(jnp.where(lane == (ids & 127), found, 0.0), axis=0, keepdims=True)
    loads[1].wait()

    def precondition(j):
        chunk = chunk_of(j)
        other_core(0, chunk)
        total = jnp.zeros((count, width), jnp.float32)
        for slot in range(8):
            total = total + lax.dot_general(
                gathered[0, slot, chunk], fisher[:, slot * width:(slot + 1) * width], NT,
                preferred_element_type=jnp.float32,
            )
        gathered[1, s, chunk] = total.astype(jnp.bfloat16)
        send_straight(chunk)

    def cross(part, tile):
        return pltpu.make_async_remote_copy(
            src_ref=sent.at[part, tile],
            dst_ref=landed.at[part, tile],
            send_sem=xsend_sem.at[part, tile],
            recv_sem=xrecv_sem.at[part, tile],
            device_id=(g, 1 - c, s),
            device_id_type=MESH,
        )

    def score(chunk, tile):
        total = jnp.zeros((count, cols), jnp.float32)
        for slot in range(8):
            total = total + lax.dot_general(
                gathered[1, slot, chunk], slab[tile * cols:(tile + 1) * cols, slot * width:(slot + 1) * width], NT,
                preferred_element_type=jnp.float32,
            )
        return total * weight[:, tile * cols:(tile + 1) * cols]

    def give(j):
        other_core(1, chunk_of(j))
        for tile in range(tiles):
            sent[j, tile] = score(chunk_of(j), tile).astype(jnp.bfloat16)
            cross(j, tile).start()

    def keep(j):
        other_core(1, chunk_of(j))
        at = slice((j - parts) * count, (j - parts + 1) * count)
        for tile in range(tiles):
            out_ref[at, tile * cols:(tile + 1) * cols] = score(chunk_of(j), tile)

    def add(j, carry):
        at = pl.ds(pl.multiple_of(j * count, count), count)
        for tile in range(tiles):
            cross(j, tile).wait_recv()
            spot = slice(tile * cols, (tile + 1) * cols)
            out_ref[at, spot] = (out_ref[at, spot] + landed[j, tile].astype(jnp.float32)) * 0.5
        return carry

    slab_here = False
    for what, j, *rest in PLAN[begin + 1:]:
        if what == "send":
            send(0, chunk_of(j))
        elif what == "query":
            relay(0, rest[0], chunk_of(j))
        elif what == "multiply":
            precondition(j)
        elif what == "relay":
            receive(rest[0], chunk_of(j))
        else:
            if not slab_here:
                loads[4].wait()
                slab_here = True
            give(j) if j < parts else keep(j)
    lax.fori_loop(0, parts, add, 0)

    def drain(t, carry):
        phase, chunk = t // (2 * parts), t % (2 * parts)

        for origin in range(4):
            across(phase, origin, chunk).wait_send()

            @pl.when((phase == 0) & (z > 0) & (origin >= z))
            def _():
                along(0, origin, chunk, 0).wait_send()

            @pl.when((phase == 0) & (z < 3) & (origin <= z))
            def _():
                along(0, origin, chunk, 1).wait_send()

        @pl.when((phase == 1) & inner)
        def _():
            straight(chunk, near).wait_send()
            straight(chunk, outer).wait_send()
            passed(chunk).wait_send()

        @pl.when((phase == 1) & jnp.logical_not(inner))
        def _():
            for dest in (far, third, near):
                straight(chunk, dest).wait_send()

        return carry

    lax.fori_loop(0, 4 * parts, drain, 0)
    for j in range(parts):
        for tile in range(tiles):
            cross(j, tile).wait_send()


def fused_body(queries, fisher_inv, slab_feats, row_ids, resid_weight):
    whole, width = queries.shape[1:]
    rows, depth, tiles, parts = slab_feats.shape[1], slab_feats.shape[2], 4, PARTS
    count = whole // (2 * parts)
    table = resid_weight.shape[1]
    hbm, vmem = pl.BlockSpec(memory_space=pl.ANY), pl.BlockSpec(memory_space=pltpu.VMEM)
    return pl.pallas_call(
        functools.partial(kernel, tiles, parts),
        out_shape=jax.ShapeDtypeStruct((whole // 2, rows), jnp.float32),
        in_specs=[hbm, hbm, hbm, hbm, hbm],
        out_specs=vmem,
        scratch_shapes=[
            pltpu.VMEM((1, rows), jnp.int32),
            pltpu.VMEM((table // 128, 128), jnp.float32),
            pltpu.VMEM((2, 8, 2 * parts, count, width), jnp.bfloat16),
            pltpu.VMEM((width, depth), jnp.bfloat16),
            pltpu.VMEM((rows, depth), jnp.bfloat16),
            pltpu.VMEM((1, rows), jnp.float32),
            pltpu.VMEM((parts, tiles, count, rows // tiles), jnp.bfloat16),
            pltpu.VMEM((parts, tiles, count, rows // tiles), jnp.bfloat16),
            pltpu.SemaphoreType.DMA((5,)),
            pltpu.SemaphoreType.DMA((2, 2, 4, 2 * parts)),
            pltpu.SemaphoreType.DMA((2, 4, 2 * parts)),
            pltpu.SemaphoreType.DMA((2, 8, 2 * parts)),
            pltpu.SemaphoreType.DMA((parts, tiles)),
            pltpu.SemaphoreType.DMA((parts, tiles)),
        ],
        compiler_params=pltpu.CompilerParams(
            collective_id=0, has_side_effects=True, vmem_limit_bytes=60 * 1024 * 1024
        ),
        cost_estimate=pl.CostEstimate(
            flops=2 * whole * depth * (width + rows), bytes_accessed=2 * depth * (width + rows), transcendentals=0
        ),
    )(
        queries.reshape(2 * parts, count, width),
        fisher_inv[0],
        slab_feats[0],
        row_ids.reshape(1, rows),
        resid_weight.reshape(table // 128, 128),
    )


def solution(mesh):
    placed = (
        P("ckpt", "groups", "store"),
        P("ckpt", "store", None),
        P("ckpt", ("groups", "store"), None),
        P(("groups", "store")),
        P("ckpt", None),
    )
    body = plain_body
    if mesh.shape["ckpt"] == 2 and mesh.shape["store"] == 8:
        body = fused_body
    return jax.shard_map(
        body, mesh=mesh, in_specs=placed, out_specs=P(("groups", "ckpt"), "store"), check_vma=False
    )
```

```python
import functools

import jax
import jax.numpy as jnp
from jax import lax
from jax.experimental import pallas as pl
from jax.experimental.pallas import tpu as pltpu
from jax.sharding import PartitionSpec as P

MESH = pl.DeviceIdType.MESH
NT = (((1,), (1,)), ((), ()))
TN = (((0,), (0,)), ((), ()))
PARTS = 2
PLAN = (
    ("send", 0),
    ("send", 1),
    ("send", 2),
    ("send", 3),
    None,
    ("query", 0, 1),
    ("query", 1, 1),
    ("query", 0, 2),
    ("query", 1, 2),
    ("query", 2, 1),
    ("query", 3, 1),
    ("query", 0, 3),
    ("query", 1, 3),
    ("multiply", 0),
    ("multiply", 1),
    ("query", 2, 2),
    ("query", 3, 2),
    ("relay", 0, 1),
    ("relay", 1, 1),
    ("query", 2, 3),
    ("query", 3, 3),
    ("multiply", 2),
    ("multiply", 3),
    ("relay", 0, 2),
    ("relay", 0, 3),
    ("score", 0),
    ("relay", 1, 2),
    ("relay", 1, 3),
    ("score", 1),
    ("relay", 2, 1),
    ("relay", 3, 1),
    ("relay", 2, 2),
    ("relay", 2, 3),
    ("relay", 3, 2),
    ("score", 2),
    ("relay", 3, 3),
    ("score", 3),
)


def plain_body(queries, fisher_inv, slab_feats, row_ids, resid_weight):
    feats = slab_feats[0]
    fisher_rows = fisher_inv[0]
    whole_queries = lax.all_gather(queries[0], "store", axis=1, tiled=True)
    own_cols = lax.dot_general(
        whole_queries, fisher_rows, NT, preferred_element_type=jnp.float32
    ).astype(jnp.bfloat16)
    partial_value = lax.dot_general(
        lax.all_gather(own_cols, "store", axis=1, tiled=True), feats, NT, preferred_element_type=jnp.float32
    )
    weights = jnp.take(resid_weight[0], row_ids, axis=0)
    weighted = partial_value * weights[None, :]
    members = lax.axis_size("ckpt")
    summed = lax.psum_scatter(weighted, "ckpt", scatter_dimension=0, tiled=True)
    return summed * (1.0 / members)


def kernel(
    tiles, parts, q_hbm, f_hbm, s_hbm, id_hbm, table_hbm, out_ref,
    id_ref, table_ref, gathered, fisher, slab, weight, sent, landed,
    local_sem, send_sem, core_sem, recv_sem, xsend_sem, xrecv_sem,
):
    g, c, s = lax.axis_index("groups"), lax.axis_index("ckpt"), lax.axis_index("store")
    z, core = s // 2, s % 2
    inner = (z == 1) | (z == 2)
    outer = jnp.where(z < 2, 0, 3)
    near = jnp.where((z == 0) | (z == 2), 1, 2)
    far = jnp.where(inner, outer, 3 - z)
    third = (z + 2) % 4
    count, width = q_hbm.shape[1:]
    cols = out_ref.shape[-1] // tiles

    loads = [
        pltpu.make_async_copy(q_hbm, gathered.at[0, s], local_sem.at[0]),
        pltpu.make_async_copy(f_hbm, fisher, local_sem.at[1]),
        pltpu.make_async_copy(id_hbm, id_ref, local_sem.at[2]),
        pltpu.make_async_copy(table_hbm, table_ref, local_sem.at[3]),
        pltpu.make_async_copy(s_hbm, slab, local_sem.at[4]),
    ]
    for load in loads:
        load.start()

    barrier = pltpu.get_barrier_semaphore()

    def greet(cc, ss):
        pl.semaphore_signal(barrier, inc=1, device_id=(g, cc, ss), device_id_type=MESH)

    greet(c, s + 1 - 2 * core)
    greet(1 - c, s)

    for d in (1, 2, 3):
        greet(c, 2 * ((z + d) % 4) + core)
    pl.semaphore_wait(barrier, 5)

    def copy(phase, slot, chunk, target, sem):
        return pltpu.make_async_remote_copy(
            src_ref=gathered.at[phase, slot, chunk],
            dst_ref=gathered.at[phase, slot, chunk],
            send_sem=sem,
            recv_sem=recv_sem.at[phase, slot, chunk],
            device_id=(g, c, target),
            device_id_type=MESH,
        )

    def along(phase, origin, chunk, way):
        return copy(phase, 2 * origin + core, chunk, s - 2 + 4 * way, send_sem.at[phase, way, origin, chunk])

    def across(phase, origin, chunk):
        return copy(phase, 2 * origin + core, chunk, s + 1 - 2 * core, core_sem.at[phase, origin, chunk])

    def arrived(phase, slot, chunk):
        copy(phase, slot, chunk, s + 1 - 2 * core, core_sem.at[phase, 0, chunk]).wait_recv()

    def send(phase, chunk):
        @pl.when(z > 0)
        def _():
            along(phase, z, chunk, 0).start()

        @pl.when(z < 3)
        def _():
            along(phase, z, chunk, 1).start()

        across(phase, z, chunk).start()

    def relay(phase, hop, chunk):
        @pl.when(z + hop < 4)
        def _():
            arrived(phase, 2 * (z + hop) + core, chunk)

            @pl.when(z > 0)
            def _():
                along(phase, z + hop, chunk, 0).start()

            across(phase, z + hop, chunk).start()

        @pl.when(z - hop >= 0)
        def _():
            arrived(phase, 2 * (z - hop) + core, chunk)

            @pl.when(z < 3)
            def _():
                along(phase, z - hop, chunk, 1).start()

            across(phase, z - hop, chunk).start()

    def straight(chunk, dest):
        return copy(1, s, chunk, 2 * dest + core, send_sem.at[1, 0, dest, chunk])

    def passed(chunk):
        return copy(1, 2 * near + core, chunk, 2 * outer + core, send_sem.at[1, 1, 0, chunk])

    def send_straight(chunk):
        @pl.when(inner)
        def _():
            straight(chunk, near).start()
            straight(chunk, outer).start()

        @pl.when(jnp.logical_not(inner))
        def _():
            straight(chunk, far).start()
            straight(chunk, third).start()
            straight(chunk, near).start()

        across(1, z, chunk).start()

    def receive(step, chunk):
        origin = (near, far, third)[step - 1]
        arrived(1, 2 * origin + core, chunk)
        if step == 1:
            @pl.when(inner)
            def _():
                passed(chunk).start()

        across(1, origin, chunk).start()

    def other_core(phase, chunk):
        for origin in range(4):
            arrived(phase, 2 * origin + 1 - core, chunk)

    def chunk_of(j):
        return jnp.where(j < parts, (1 - c) * parts + j, c * parts + j - parts)

    loads[0].wait()

    begin = PLAN.index(None)
    for what, j, *rest in PLAN[:begin]:
        send(0, chunk_of(j))

    loads[2].wait()
    loads[3].wait()
    ids = id_ref[...]
    rows = table_ref.shape[0]
    picked = jnp.where(
        lax.broadcasted_iota(jnp.int32, (rows, ids.shape[1]), 0) == lax.shift_right_logical(ids, 7), 1.0, 0.0
    ).astype(jnp.bfloat16)
    rest = table_ref[...]
    found = jnp.zeros((128, ids.shape[1]), jnp.float32)
    for _ in range(3):
        piece = rest.astype(jnp.bfloat16)
        found = found + lax.dot_general(piece, picked, TN, preferred_element_type=jnp.float32)
        rest = rest - piece.astype(jnp.float32)
    lane = lax.broadcasted_iota(jnp.int32, found.shape, 0)
    weight[...] = jnp.sum(jnp.where(lane == (ids & 127), found, 0.0), axis=0, keepdims=True)
    loads[1].wait()

    def precondition(j):
        chunk = chunk_of(j)
        other_core(0, chunk)
        total = jnp.zeros((count, width), jnp.float32)
        for slot in range(8):
            total = total + lax.dot_general(
                gathered[0, slot, chunk], fisher[:, slot * width:(slot + 1) * width], NT,
                preferred_element_type=jnp.float32,
            )
        gathered[1, s, chunk] = total.astype(jnp.bfloat16)
        send_straight(chunk)

    def cross(part, tile):
        return pltpu.make_async_remote_copy(
            src_ref=sent.at[part, tile],
            dst_ref=landed.at[part, tile],
            send_sem=xsend_sem.at[part, tile],
            recv_sem=xrecv_sem.at[part, tile],
            device_id=(g, 1 - c, s),
            device_id_type=MESH,
        )

    def score(chunk, tile):
        total = jnp.zeros((count, cols), jnp.float32)
        for slot in range(8):
            total = total + lax.dot_general(
                gathered[1, slot, chunk], slab[tile * cols:(tile + 1) * cols, slot * width:(slot + 1) * width], NT,
                preferred_element_type=jnp.float32,
            )
        return total * weight[:, tile * cols:(tile + 1) * cols]

    def give(j):
        other_core(1, chunk_of(j))
        for tile in range(tiles):
            sent[j, tile] = score(chunk_of(j), tile).astype(jnp.bfloat16)
            cross(j, tile).start()

    def keep(j):
        other_core(1, chunk_of(j))
        at = slice((j - parts) * count, (j - parts + 1) * count)
        for tile in range(tiles):
            out_ref[at, tile * cols:(tile + 1) * cols] = score(chunk_of(j), tile)

    def add(j, carry):
        at = pl.ds(pl.multiple_of(j * count, count), count)
        for tile in range(tiles):
            cross(j, tile).wait_recv()
            spot = slice(tile * cols, (tile + 1) * cols)
            out_ref[at, spot] = (out_ref[at, spot] + landed[j, tile].astype(jnp.float32)) * 0.5
        return carry

    slab_here = False
    for what, j, *rest in PLAN[begin + 1:]:
        if what == "send":
            send(0, chunk_of(j))
        elif what == "query":
            relay(0, rest[0], chunk_of(j))
        elif what == "multiply":
            precondition(j)
        elif what == "relay":
            receive(rest[0], chunk_of(j))
        else:
            if not slab_here:
                loads[4].wait()
                slab_here = True
            give(j) if j < parts else keep(j)
    lax.fori_loop(0, parts, add, 0)

    def drain(t, carry):
        phase, chunk = t // (2 * parts), t % (2 * parts)

        for origin in range(4):
            across(phase, origin, chunk).wait_send()

            @pl.when((phase == 0) & (z > 0) & (origin >= z))
            def _():
                along(0, origin, chunk, 0).wait_send()

            @pl.when((phase == 0) & (z < 3) & (origin <= z))
            def _():
                along(0, origin, chunk, 1).wait_send()

        @pl.when((phase == 1) & inner)
        def _():
            straight(chunk, near).wait_send()
            straight(chunk, outer).wait_send()
            passed(chunk).wait_send()

        @pl.when((phase == 1) & jnp.logical_not(inner))
        def _():
            for dest in (far, third, near):
                straight(chunk, dest).wait_send()

        return carry

    lax.fori_loop(0, 4 * parts, drain, 0)
    for j in range(parts):
        for tile in range(tiles):
            cross(j, tile).wait_send()


def fused_body(queries, fisher_inv, slab_feats, row_ids, resid_weight):
    whole, width = queries.shape[1:]
    rows, depth, tiles, parts = slab_feats.shape[1], slab_feats.shape[2], 2, PARTS
    count = whole // (2 * parts)
    table = resid_weight.shape[1]
    hbm, vmem = pl.BlockSpec(memory_space=pl.ANY), pl.BlockSpec(memory_space=pltpu.VMEM)
    return pl.pallas_call(
        functools.partial(kernel, tiles, parts),
        out_shape=jax.ShapeDtypeStruct((whole // 2, rows), jnp.float32),
        in_specs=[hbm, hbm, hbm, hbm, hbm],
        out_specs=vmem,
        scratch_shapes=[
            pltpu.VMEM((1, rows), jnp.int32),
            pltpu.VMEM((table // 128, 128), jnp.float32),
            pltpu.VMEM((2, 8, 2 * parts, count, width), jnp.bfloat16),
            pltpu.VMEM((width, depth), jnp.bfloat16),
            pltpu.VMEM((rows, depth), jnp.bfloat16),
            pltpu.VMEM((1, rows), jnp.float32),
            pltpu.VMEM((parts, tiles, count, rows // tiles), jnp.bfloat16),
            pltpu.VMEM((parts, tiles, count, rows // tiles), jnp.bfloat16),
            pltpu.SemaphoreType.DMA((5,)),
            pltpu.SemaphoreType.DMA((2, 2, 4, 2 * parts)),
            pltpu.SemaphoreType.DMA((2, 4, 2 * parts)),
            pltpu.SemaphoreType.DMA((2, 8, 2 * parts)),
            pltpu.SemaphoreType.DMA((parts, tiles)),
            pltpu.SemaphoreType.DMA((parts, tiles)),
        ],
        compiler_params=pltpu.CompilerParams(
            collective_id=0, has_side_effects=True, vmem_limit_bytes=60 * 1024 * 1024
        ),
        cost_estimate=pl.CostEstimate(
            flops=2 * whole * depth * (width + rows), bytes_accessed=2 * depth * (width + rows), transcendentals=0
        ),
    )(
        queries.reshape(2 * parts, count, width),
        fisher_inv[0],
        slab_feats[0],
        row_ids.reshape(1, rows),
        resid_weight.reshape(table // 128, 128),
    )


def solution(mesh):
    placed = (
        P("ckpt", "groups", "store"),
        P("ckpt", "store", None),
        P("ckpt", ("groups", "store"), None),
        P(("groups", "store")),
        P("ckpt", None),
    )
    body = plain_body
    if mesh.shape["ckpt"] == 2 and mesh.shape["store"] == 8:
        body = fused_body
    return jax.shard_map(
        body, mesh=mesh, in_specs=placed, out_specs=P(("groups", "ckpt"), "store"), check_vma=False
    )
```
